128 devices in a mesh: dp: 8 (over z, y_lo), expert: 16 (over y_hi, x, core).
Axes of the slice: x: 4, y: 4 (y_hi: 2, y_lo: 2; y = y_hi * 2 + y_lo), z: 4, core: 2. Of those that a mesh axis runs over, the one named last changes fastest.
Arguments:
- tokens_in: bfloat16 [16384, 2560], P(('dp', 'expert')), may hold values from -6 to 6
- out_grad: bfloat16 [16384, 2560], P(('dp', 'expert')), may hold values from -6 to 6
- expert_ids: int32 [16384, 6], P(('dp', 'expert')), may hold values from 0 to 15, as said below
- route_probs: bfloat16 [16384, 6], P(('dp', 'expert')), may hold values from 0.019897461 to 0.5
- weights_in: float32 [16, 2560, 1536], P('expert', 'dp'), may hold values from -0.125 to 0.125
- weights_out: float32 [16, 768, 2560], P('expert', 'dp'), may hold values from -0.21875 to 0.21875
- first_in: float32 [16, 2560, 1536], P('expert', 'dp'), may hold values from -24 to 24
- first_out: float32 [16, 768, 2560], P('expert', 'dp'), may hold values from -24 to 24
- second_in: float32 [16, 2560, 1536], P('expert', 'dp'), may hold values from 1 to 100
- second_out: float32 [16, 768, 2560], P('expert', 'dp'), may hold values from 1 to 100
Outputs:
- input_grad: bfloat16 [16384, 2560], P(('dp', 'expert'))
- route_grad: bfloat16 [16384, 6], P(('dp', 'expert'))
- new_weights_in: float32 [16, 2560, 1536], P('expert', 'dp')
- new_weights_out: float32 [16, 768, 2560], P('expert', 'dp')
- new_first_in: float32 [16, 2560, 1536], P('expert', 'dp')
- new_first_out: float32 [16, 768, 2560], P('expert', 'dp')
- new_second_in: float32 [16, 2560, 1536], P('expert', 'dp')
- new_second_out: float32 [16, 768, 2560], P('expert', 'dp')
The draws below stay inside these ranges and needn't reach their ends.
Inputs may be any that keep to these rules, and one draw needn't show every extreme that they name: `expert_ids`: each row names 6 different experts. Among the rows of one device no expert is named more than 54 times, and in every group of 16 devices that share a dp index one expert is named exactly 54 times by each device of the group.
All inputs are finite; a program needn't handle non-finite values.
Results may differ from the reference program's by a relative error of at most 0.025.
Values may be sent and summed in bfloat16 or wider, within the bound.
No kernel may reach another device: no remote copies, remote signals or barrier semaphores. Data moves between devices by JAX's collectives and lax.ppermute only.
A program may use at most 128 MiB of HBM per device.

```python
import math
import jax
import jax.numpy as jnp
from jax import lax

D = 2560
FF = 768
TOPK = 6
TOK_DEV = 128
EXPERTS = 16
CAP = 54
TOKENS = 16384


def draw_expert_ids(key, part):
    blocks = TOKENS // TOK_DEV
    groups = blocks // EXPERTS
    slot_total = EXPERTS * CAP
    filled = TOK_DEV * TOPK
    hot_key, block_key = jax.random.split(key)
    hot_experts = jnp.repeat(jax.random.randint(hot_key, (groups,), 0, EXPERTS).astype(jnp.int32), EXPERTS)
    block_keys = jax.random.split(block_key, blocks)
    slot_expert = jnp.arange(slot_total, dtype=jnp.int32) // CAP
    slot_number = jnp.arange(slot_total, dtype=jnp.int32)

    def one_block(one_key, hot_expert):
        order_key, token_key = jax.random.split(one_key)
        ranking = jax.random.permutation(order_key, slot_total).astype(jnp.int32)
        scores = jnp.where(slot_expert == hot_expert, slot_number - slot_total, ranking)
        chosen = jnp.sort(jnp.argsort(scores, stable=True)[:filled].astype(jnp.int32))
        listed = (chosen // CAP).reshape(TOPK, TOK_DEV).T
        return listed[jax.random.permutation(token_key, TOK_DEV)]
    return jax.vmap(one_block)(block_keys, hot_experts).reshape(TOKENS, TOPK).astype(jnp.int32)


def block_scale(key, dims, shards, smallest, high):
    level, own = 1.0, jax.random.fold_in(key, 6)
    for dim, parts in shards:
        heights = jnp.exp(jax.random.uniform(jax.random.fold_in(own, dim), (parts,), jnp.float32, smallest / len(shards), high / len(shards)))
        level = level * jnp.repeat(heights, dims[dim] // parts).reshape([-1 if axis == dim else 1 for axis in range(len(dims))])
    return level


def centred(stream_key, shape, spread, limit, cuts=(), kind=jnp.bfloat16):
    drawn = spread * jax.random.normal(stream_key, shape, jnp.float32)
    if cuts:
        drawn = drawn * block_scale(stream_key, shape, cuts, -0.22, 0.18)
    return jnp.clip(drawn, -limit, limit).astype(kind)


def setup_inputs(seed: int = 0) -> dict:
    keys = jax.random.split(jax.random.key(seed), 11)
    return {
        "tokens_in": centred(keys[0], (TOKENS, D), 1.0, 6.0, ((0, 128),)),
        "out_grad": centred(keys[1], (TOKENS, D), 1.0, 6.0, ((0, 128),)),
        "expert_ids": draw_expert_ids(jax.random.fold_in(keys[10], 71), 0),
        "route_probs": jnp.clip(jnp.exp(math.log(0.5) - 3.224016 * jax.random.uniform(keys[3], (TOKENS, TOPK), jnp.float32) ** block_scale(keys[3], (TOKENS, TOPK), ((0, 128),), -0.2, 0.2)), 0.019897461, 0.5).astype(jnp.bfloat16),
        "weights_in": centred(keys[4], (EXPERTS, D, 2 * FF), D ** -0.5, 0.125, ((0, 16), (1, 8)), jnp.float32),
        "weights_out": centred(keys[5], (EXPERTS, FF, D), FF ** -0.5, 0.21875, ((0, 16), (1, 8)), jnp.float32),
        "first_in": centred(keys[6], (EXPERTS, D, 2 * FF), 4.0, 24.0, ((0, 16), (1, 8)), jnp.float32),
        "first_out": centred(keys[7], (EXPERTS, FF, D), 4.0, 24.0, ((0, 16), (1, 8)), jnp.float32),
        "second_in": jnp.clip(jnp.exp(math.log(100.0) - 4.6051702 * jax.random.uniform(keys[8], (EXPERTS, D, 2 * FF), jnp.float32) ** block_scale(keys[8], (EXPERTS, D, 2 * FF), ((0, 16), (1, 8)), -0.2, 0.2)), 1.0, 100.0),
        "second_out": jnp.clip(jnp.exp(math.log(100.0) - 4.6051702 * jax.random.uniform(keys[9], (EXPERTS, FF, D), jnp.float32) ** block_scale(keys[9], (EXPERTS, FF, D), ((0, 16), (1, 8)), -0.2, 0.2)), 1.0, 100.0),
    }


beta_one = 0.9
beta_two = 0.95
learn_rate = 0.00024
decay_rate = 0.1
adam_eps = 1e-08
adam_step = 100.0

def silu_parts(gate_value):
    sigmoid_value = jax.nn.sigmoid(gate_value)
    return (gate_value * sigmoid_value, sigmoid_value * (1.0 + gate_value * (1.0 - sigmoid_value)))

def expert_rows(token_block, grad_block, prob_block, wide_in, wide_out):
    hidden = wide_out.shape[0]
    preact = jnp.dot(token_block, wide_in, preferred_element_type=jnp.float32)
    gate_value = preact[:, :hidden]
    up_value = preact[:, hidden:]
    silu_gate, silu_slope = silu_parts(gate_value)
    activation = silu_gate * up_value
    back_proj = jnp.dot(grad_block, wide_out.T, preferred_element_type=jnp.float32)
    route_part = lax.optimization_barrier(jnp.sum(activation * back_proj, axis=1)).astype(jnp.bfloat16)
    weight = prob_block.astype(jnp.float32)[:, None]
    act_grad = weight * back_proj
    pre_grad = jnp.concatenate([act_grad * up_value * silu_slope, act_grad * silu_gate], axis=1).astype(jnp.bfloat16)
    scaled = (weight * activation).astype(jnp.bfloat16)
    row_grad = jnp.dot(pre_grad, wide_in.T, preferred_element_type=jnp.float32).astype(jnp.bfloat16)
    return (row_grad, route_part, pre_grad, scaled)

def adam_update(weights, first, second, grad):
    first_new = beta_one * first + (1.0 - beta_one) * grad
    second_new = beta_two * second + (1.0 - beta_two) * grad * grad
    fix_one = 1.0 - beta_one ** adam_step
    fix_two = 1.0 - beta_two ** adam_step
    step_size = first_new / fix_one / (jnp.sqrt(second_new / fix_two) + adam_eps)
    return (weights - learn_rate * (step_size + decay_rate * weights), first_new, second_new)

def reference(tokens_in, out_grad, expert_ids, route_probs, weights_in, weights_out, first_in, first_out, second_in, second_out):
    groups = TOKENS // (TOK_DEV * EXPERTS)
    group_picks = TOK_DEV * EXPERTS * TOPK
    group_rows = EXPERTS * CAP
    pick_total = TOKENS * TOPK
    flat_ids = expert_ids.reshape(groups, group_picks).astype(jnp.int32)
    expert_range = jnp.arange(EXPERTS, dtype=jnp.int32)
    onehot = (flat_ids[:, :, None] == expert_range[None, None, :]).astype(jnp.int32)
    slot_rank = lax.optimization_barrier(jnp.sum((jnp.cumsum(onehot, axis=1) - onehot) * onehot, axis=2)).astype(jnp.int32)
    group_index = jnp.broadcast_to(jnp.arange(groups, dtype=jnp.int32)[:, None], (groups, group_picks))
    pick_index = jnp.arange(pick_total, dtype=jnp.int32).reshape(groups, group_picks)
    slot_table = jnp.full((EXPERTS, groups, group_rows), pick_total, jnp.int32)
    slot_table = slot_table.at[flat_ids, group_index, slot_rank].set(pick_index)
    zero_row = jnp.zeros((1, D), tokens_in.dtype)
    padded_tokens = jnp.concatenate([tokens_in, zero_row], axis=0)
    padded_grads = jnp.concatenate([out_grad, zero_row], axis=0)
    padded_probs = jnp.concatenate([route_probs.reshape(-1), jnp.zeros((1,), route_probs.dtype)])
    wide_in = weights_in.astype(jnp.bfloat16)
    wide_out = weights_out.astype(jnp.bfloat16)

    def per_expert(carried, expert):
        input_acc, route_acc = carried
        picks_here = slot_table[expert]
        wide_in_e = wide_in[expert]
        wide_out_e = wide_out[expert]

        def per_group(slot_picks):
            token_rows = (slot_picks // TOPK).astype(jnp.int32)
            token_block = padded_tokens[token_rows]
            grad_block = padded_grads[token_rows]
            prob_block = padded_probs[slot_picks]
            row_grad, route_part, pre_grad, scaled = expert_rows(token_block, grad_block, prob_block, wide_in_e, wide_out_e)
            part_in = jnp.dot(token_block.T, pre_grad, preferred_element_type=jnp.float32).astype(jnp.bfloat16)
            part_out = jnp.dot(scaled.T, grad_block, preferred_element_type=jnp.float32).astype(jnp.bfloat16)
            return (row_grad, route_part, part_in, part_out)
        row_grad, route_part, part_in, part_out = lax.map(per_group, picks_here)
        flat_picks = picks_here.reshape(-1)
        input_acc = input_acc.at[(flat_picks // TOPK).astype(jnp.int32)].add(row_grad.reshape(-1, D).astype(jnp.float32))
        route_acc = route_acc.at[flat_picks].add(route_part.reshape(-1).astype(jnp.float32))
        grad_in = lax.optimization_barrier(jnp.sum(part_in.astype(jnp.float32), axis=0))
        grad_out = lax.optimization_barrier(jnp.sum(part_out.astype(jnp.float32), axis=0))
        return ((input_acc, route_acc), (grad_in, grad_out))
    start_acc = (jnp.zeros((TOKENS + 1, D), jnp.float32), jnp.zeros((pick_total + 1,), jnp.float32))
    (input_acc, route_acc), (grad_in, grad_out) = lax.scan(per_expert, start_acc, expert_range)
    new_weights_in, new_first_in, new_second_in = adam_update(weights_in, first_in, second_in, grad_in)
    new_weights_out, new_first_out, new_second_out = adam_update(weights_out, first_out, second_out, grad_out)
    input_grad = input_acc[:TOKENS].astype(jnp.bfloat16)
    route_grad = route_acc[:pick_total].reshape(TOKENS, TOPK).astype(jnp.bfloat16)
    return (input_grad, route_grad, new_weights_in, new_weights_out, new_first_in, new_first_out, new_second_in, new_second_out)
```

```python
import functools

import jax
import jax.numpy as jnp
from jax import lax
from jax.experimental import pallas as pl
from jax.experimental.pallas import tpu as pltpu
from jax.sharding import PartitionSpec as P

beta_one = 0.9
beta_two = 0.95
learn_rate = 0.00024
decay_rate = 0.1
adam_eps = 1e-08
adam_step = 100.0

ring = 4


def adam_update(weights, first, second, grad):
    first_new = beta_one * first + (1.0 - beta_one) * grad
    second_new = beta_two * second + (1.0 - beta_two) * grad * grad
    fix_one = 1.0 - beta_one**adam_step
    fix_two = 1.0 - beta_two**adam_step
    step_size = first_new / fix_one / (jnp.sqrt(second_new / fix_two) + adam_eps)
    return (weights - learn_rate * (step_size + decay_rate * weights), first_new, second_new)


def dp_at(index, dz, dy):
    return (index // 2 + dz) % ring * 2 + (index % 2 + dy) % 2


def dp_send(value, dz, dy):
    return lax.ppermute(value, "dp", [(i, dp_at(i, dz, dy)) for i in range(2 * ring)])


def ex_at(index, dy, dx, dc):
    return (index // 8 + dy) % 2 * 8 + (index // 2 + dx) % ring * 2 + (index + dc) % 2


def ex_send(value, dy, dx, dc):
    return lax.ppermute(value, "expert", [(i, ex_at(i, dy, dx, dc)) for i in range(4 * ring)])


def after(value, *others):
    return lax.optimization_barrier((value, *others))[0]


def ring_all(shard, send):
    half = shard.shape[0] // 2
    behind, ahead = send(shard, 1), send(shard, -1)
    far_low, far_high = send(behind[:half], 1), send(ahead[half:], -1)
    return [(0, 0, shard), (-1, 0, behind), (1, 0, ahead), (2, 0, far_low), (2, half, far_high)]


def gather_weights(shard):
    mine = lax.axis_index("dp")
    rows = shard.shape[0]
    other = dp_send(shard, 0, 1)
    own_side = ring_all(shard, lambda v, d: dp_send(v, d, 0))
    other_side = ring_all(other, lambda v, d: dp_send(v, d, 0))
    whole = jnp.zeros((2 * ring * rows, shard.shape[1]), shard.dtype)
    for dy, side in ((0, own_side), (1, other_side)):
        for dz, low, piece in side:
            place = dp_at(mine, dz, dy) * rows + low
            whole = lax.dynamic_update_slice(whole, piece, (place, 0))
    return whole, (other_side[1][2], other_side[2][2])


def gather_tokens(shard):
    other = ex_send(shard, 1, 0, 0)
    pieces = []
    for dy, start in ((0, shard), (1, other)):
        for dx, low, piece in ring_all(start, lambda v, d: ex_send(v, 0, d, 0)):
            pieces.append((dy, dx, 0, low, piece))
    late = (pieces[6][4], pieces[7][4])
    pieces += [(dy, dx, 1, low, ex_send(piece, 0, 0, 1)) for dy, dx, _, low, piece in pieces]
    return pieces, late


def pick_kernel(lows, place_ref, prob_ref, rank_ref, *refs):
    count = len(lows)
    pieces, (out_ref, held, sems) = refs[:count], refs[count:]
    copies = []
    for i, (low, piece) in enumerate(zip(lows, pieces)):
        copies.append(
            pltpu.make_async_copy(
                piece, held.at[place_ref[i], pl.ds(low, piece.shape[0])], sems.at[i]
            )
        )
    for copy in copies:
        copy.start()
    for copy in copies:
        copy.wait()
    sources, slots, _ = out_ref.shape
    slot = lax.broadcasted_iota(jnp.int32, (slots, held.shape[1]), 0).astype(jnp.float32)
    for s in range(sources):
        chosen = (rank_ref[s : s + 1, :] == slot) & (prob_ref[s : s + 1, :] > 0.0)
        chosen = jnp.where(chosen, 1.0, 0.0).astype(jnp.bfloat16)
        out_ref[s] = jnp.dot(chosen, held[s], preferred_element_type=jnp.float32).astype(
            jnp.bfloat16
        )


def pick_rows(pieces, probs, ranks, slots):
    mine = lax.axis_index("expert")
    places = jnp.stack([ex_at(mine, dy, dx, dc) for dy, dx, dc, _, _ in pieces]).astype(jnp.int32)
    lows = tuple(low for _, _, _, low, _ in pieces)
    arrays = [piece for *_, piece in pieces]
    sources, tokens = probs.shape
    features = arrays[0].shape[1]
    return pl.pallas_call(
        functools.partial(pick_kernel, lows),
        out_shape=jax.ShapeDtypeStruct((sources, slots, features), jnp.bfloat16),
        in_specs=[pl.BlockSpec(memory_space=pltpu.SMEM)]
        + [pl.BlockSpec(memory_space=pltpu.VMEM)] * 2
        + [pl.BlockSpec(memory_space=pl.ANY)] * len(arrays),
        out_specs=pl.BlockSpec(memory_space=pltpu.VMEM),
        scratch_shapes=[
            pltpu.VMEM((sources, tokens, features), jnp.bfloat16),
            pltpu.SemaphoreType.DMA((len(arrays),)),
        ],
        compiler_params=pltpu.CompilerParams(vmem_limit_bytes=40 * 2**20),
        cost_estimate=pl.CostEstimate(
            flops=2 * sources * slots * tokens * features,
            bytes_accessed=2 * sources * (slots + tokens) * features,
            transcendentals=0,
        ),
    )(places, probs, ranks, *arrays)


def scatter_sum(part):
    mine = lax.axis_index("dp")
    rows = part.shape[0] // (2 * ring)
    half = rows // 2

    def chunk(dz, dy, low=0, count=rows):
        place = dp_at(mine, dz, dy) * rows + low
        return lax.dynamic_slice(part, (place, 0), (count, part.shape[1]))

    def wide(value):
        return value.astype(jnp.float32)

    sums = []
    for dy in (1, 0):
        far_low = dp_send(chunk(2, dy, 0, half), 1, 0)
        far_high = dp_send(chunk(2, dy, half, half), -1, 0)
        up_low = (wide(chunk(1, dy, 0, half)) + wide(far_low)).astype(jnp.bfloat16)
        up = jnp.concatenate([up_low, chunk(1, dy, half, half)], axis=0)
        down_high = (wide(chunk(-1, dy, half, half)) + wide(far_high)).astype(jnp.bfloat16)
        down = jnp.concatenate([chunk(-1, dy, 0, half), down_high], axis=0)
        from_behind, from_ahead = dp_send(up, 1, 0), dp_send(down, -1, 0)
        sums.append(wide(chunk(0, dy)) + wide(from_behind) + wide(from_ahead))
    return sums[1] + wide(dp_send(sums[0].astype(jnp.bfloat16), 0, 1))


def on_device(
    tokens_in,
    out_grad,
    expert_ids,
    route_probs,
    weights_in,
    weights_out,
    first_in,
    first_out,
    second_in,
    second_out,
):
    experts = lax.axis_size("expert")
    token_count, top_count = expert_ids.shape
    features = tokens_in.shape[1]
    hidden = weights_out.shape[1] * lax.axis_size("dp")
    capacity = 9 * token_count * top_count // (8 * experts)
    slots = -(-capacity // 8) * 8
    f32, bf16 = jnp.float32, jnp.bfloat16

    chose = expert_ids.T[:, None, :] == jnp.arange(experts, dtype=jnp.int32)[None, :, None]
    sent_probs = jnp.sum(jnp.where(chose, route_probs.T[:, None, :].astype(f32), 0.0), axis=0)
    before = (
        jnp.arange(token_count)[:, None] < jnp.arange(token_count)[None, :]
    ).astype(bf16)

    def rank_of(probs):
        return jnp.dot((probs > 0.0).astype(bf16), before, preferred_element_type=f32)

    def chosen_of(probs):
        slot = jnp.arange(slots, dtype=jnp.int32).astype(f32)[None, :, None]
        return (rank_of(probs)[:, None, :] == slot) & (probs[:, None, :] > 0.0)

    wide_in, late_in = gather_weights(weights_in[0].astype(bf16))
    token_pieces, late_tokens = gather_tokens(tokens_in)
    got_probs = lax.all_to_all(
        sent_probs.astype(bf16), "expert", split_axis=0, concat_axis=0, tiled=True
    ).astype(f32)
    wide_out, _ = gather_weights(after(weights_out[0].astype(bf16), *late_in))
    grad_pieces, _ = gather_tokens(after(out_grad, *late_tokens))

    ranks = rank_of(got_probs)
    row_total = experts * slots
    rows = pick_rows(token_pieces, got_probs, ranks, slots).reshape(row_total, features)
    weight = jnp.sum(
        jnp.where(chosen_of(got_probs), got_probs[:, None, :], 0.0), axis=2
    ).reshape(row_total, 1)
    preact = jnp.dot(rows, wide_in, preferred_element_type=f32)
    gate_value, up_value = preact[:, :hidden], preact[:, hidden:]
    gate_sigmoid = jax.nn.sigmoid(gate_value)
    silu_gate = gate_value * gate_sigmoid
    silu_slope = gate_sigmoid * (1.0 + gate_value * (1.0 - gate_sigmoid))
    activation = silu_gate * up_value
    scaled = (weight * activation).astype(bf16)

    grads = pick_rows(grad_pieces, got_probs, ranks, slots).reshape(row_total, features)
    part_out = lax.dot_general(
        scaled, grads, (((0,), (0,)), ((), ())), preferred_element_type=f32
    ).astype(bf16)
    grad_out = scatter_sum(part_out)

    back_proj = lax.dot_general(
        grads, wide_out, (((1,), (1,)), ((), ())), preferred_element_type=f32
    )
    route_part = jnp.sum(activation * back_proj, axis=1).astype(bf16)
    act_grad = weight * back_proj
    pre_grad = jnp.concatenate(
        [act_grad * up_value * silu_slope, act_grad * silu_gate], axis=1
    ).astype(bf16)
    row_grad = lax.dot_general(
        pre_grad, wide_in, (((1,), (1,)), ((), ())), preferred_element_type=f32
    ).astype(bf16)
    back_rows = lax.all_to_all(
        row_grad.reshape(experts, slots, features),
        "expert",
        split_axis=0,
        concat_axis=0,
        tiled=True,
    )
    back_route = lax.all_to_all(
        route_part.reshape(experts, slots), "expert", split_axis=0, concat_axis=0, tiled=True
    ).astype(f32)
    part_in = lax.dot_general(
        rows, pre_grad, (((0,), (0,)), ((), ())), preferred_element_type=f32
    ).astype(bf16)
    grad_in = scatter_sum(part_in)

    new_weights_out, new_first_out, new_second_out = adam_update(
        weights_out, first_out, second_out, grad_out[None]
    )
    new_weights_in, new_first_in, new_second_in = adam_update(
        weights_in, first_in, second_in, grad_in[None]
    )

    own_chosen = chosen_of(sent_probs)
    input_grad = lax.dot_general(
        own_chosen.astype(bf16).reshape(row_total, token_count),
        back_rows.reshape(row_total, features),
        (((0,), (0,)), ((), ())),
        preferred_element_type=f32,
    ).astype(bf16)
    by_token = jnp.sum(jnp.where(own_chosen, back_route[:, :, None], 0.0), axis=1)
    route_grad = jnp.sum(jnp.where(chose, by_token[None], 0.0), axis=1).T.astype(bf16)
    return (
        input_grad,
        route_grad,
        new_weights_in,
        new_weights_out,
        new_first_in,
        new_first_out,
        new_second_in,
        new_second_out,
    )


def solution(mesh):
    rows = P(("dp", "expert"), None)
    state = P("expert", "dp", None)
    return jax.shard_map(
        on_device,
        mesh=mesh,
        in_specs=(rows,) * 4 + (state,) * 6,
        out_specs=(rows,) * 2 + (state,) * 6,
        check_vma=False,
    )
```

```python
import jax
import jax.numpy as jnp
from jax import lax
from jax.sharding import PartitionSpec as P

beta_one = 0.9
beta_two = 0.95
learn_rate = 0.00024
decay_rate = 0.1
adam_eps = 1e-08
adam_step = 100.0

ring = 4


def adam_update(weights, first, second, grad):
    first_new = beta_one * first + (1.0 - beta_one) * grad
    second_new = beta_two * second + (1.0 - beta_two) * grad * grad
    fix_one = 1.0 - beta_one**adam_step
    fix_two = 1.0 - beta_two**adam_step
    step_size = first_new / fix_one / (jnp.sqrt(second_new / fix_two) + adam_eps)
    return (weights - learn_rate * (step_size + decay_rate * weights), first_new, second_new)


def dp_at(index, dz, dy):
    return (index // 2 + dz) % ring * 2 + (index % 2 + dy) % 2


def dp_send(value, dz, dy):
    return lax.ppermute(value, "dp", [(i, dp_at(i, dz, dy)) for i in range(2 * ring)])


def ex_at(index, dy, dx, dc):
    return (index // 8 + dy) % 2 * 8 + (index // 2 + dx) % ring * 2 + (index + dc) % 2


def ex_send(value, dy, dx, dc):
    return lax.ppermute(value, "expert", [(i, ex_at(i, dy, dx, dc)) for i in range(4 * ring)])


def after(value, *others):
    return lax.optimization_barrier((value, *others))[0]


def along_z(value, step):
    return dp_send(value, step, 0)


def across_low(value):
    return dp_send(value, 0, 1)


def in_order(pieces):
    mine = lax.axis_index("dp")
    rows, columns = pieces[0][2].shape
    whole = jnp.zeros((2 * ring * rows, columns), pieces[0][2].dtype)
    for dz, dy, piece in pieces:
        whole = lax.dynamic_update_slice(whole, piece, (dp_at(mine, dz, dy) * rows, 0))
    return whole


def wide(value):
    return value.astype(jnp.float32)


def narrow(value):
    return value.astype(jnp.bfloat16)


def chunk(part, dz, dy, piece=None):
    rows = part.shape[0] // (2 * ring)
    place = dp_at(lax.axis_index("dp"), dz, dy) * rows
    if piece is not None:
        rows = rows // 2
        place = place + piece * rows
    return lax.dynamic_slice(part, (place, 0), (rows, part.shape[1]))


def far_halves(part, dy):
    return along_z(chunk(part, 2, dy, 0), 1), along_z(chunk(part, 2, dy, 1), -1)


def near_sums(part, dy, halves):
    up = jnp.concatenate(
        [narrow(wide(chunk(part, 1, dy, 0)) + wide(halves[0])), chunk(part, 1, dy, 1)], axis=0
    )
    down = jnp.concatenate(
        [chunk(part, -1, dy, 0), narrow(wide(chunk(part, -1, dy, 1)) + wide(halves[1]))], axis=0
    )
    return up, down


def on_device(
    tokens_in,
    out_grad,
    expert_ids,
    route_probs,
    weights_in,
    weights_out,
    first_in,
    first_out,
    second_in,
    second_out,
):
    experts = lax.axis_size("expert")
    token_count, top_count = expert_ids.shape
    features = tokens_in.shape[1]
    hidden = weights_out.shape[1] * lax.axis_size("dp")
    capacity = 9 * token_count * top_count // (8 * experts)
    slots = -(-capacity // 8) * 8
    f32, bf16 = jnp.float32, jnp.bfloat16

    chose = expert_ids.T[:, None, :] == jnp.arange(experts, dtype=jnp.int32)[None, :, None]
    sent_probs = jnp.sum(jnp.where(chose, route_probs.T[:, None, :].astype(f32), 0.0), axis=0)
    before = (
        jnp.arange(token_count)[:, None] < jnp.arange(token_count)[None, :]
    ).astype(bf16)

    def chosen_of(probs):
        rank = jnp.dot((probs > 0.0).astype(bf16), before, preferred_element_type=f32)
        slot = jnp.arange(slots, dtype=jnp.int32).astype(f32)[None, :, None]
        return (rank[:, None, :] == slot) & (probs[:, None, :] > 0.0)

    lanes = 128
    table = jnp.pad(sent_probs.astype(bf16).T, ((0, 0), (0, lanes - experts)))
    row_total = experts * slots
    own_chosen = chosen_of(sent_probs)
    own_rows = own_chosen.astype(bf16).reshape(row_total, token_count)

    def exchange(values):
        picked = jnp.dot(own_rows, values, preferred_element_type=f32).astype(bf16)
        picked = picked.reshape(experts, slots, values.shape[1])
        return lax.all_to_all(picked, "expert", split_axis=0, concat_axis=0, tiled=True)

    rows = exchange(jnp.concatenate([tokens_in, table], axis=1))

    barrier = lax.optimization_barrier
    own_in, own_out = weights_in[0].astype(bf16), weights_out[0].astype(bf16)
    in_side, in_far = across_low(own_in), along_z(own_in, 2)
    in_behind, in_ahead = along_z(own_in, 1), along_z(own_in, -1)
    in_far, in_behind, in_ahead, own_out = barrier((in_far, in_behind, in_ahead, own_out))
    out_far, out_behind, out_ahead = along_z(own_out, 2), along_z(own_out, 1), along_z(own_out, -1)
    in_side, out_far, out_behind, out_ahead, own_out, rows, out_grad = barrier(
        (in_side, out_far, out_behind, out_ahead, own_out, rows, out_grad)
    )
    grads = exchange(out_grad).reshape(row_total, features)
    in_side_far, out_side = along_z(in_side, 2), across_low(own_out)
    in_side_behind, in_side_ahead = along_z(in_side, 1), along_z(in_side, -1)
    in_side_far, in_side_behind, in_side_ahead, out_side = barrier(
        (in_side_far, in_side_behind, in_side_ahead, out_side)
    )
    out_side_far = along_z(out_side, 2)
    out_side_behind, out_side_ahead = along_z(out_side, 1), along_z(out_side, -1)
    wide_in = in_order(
        (
            (0, 0, own_in),
            (0, 1, in_side),
            (-1, 0, in_behind),
            (1, 0, in_ahead),
            (2, 0, in_far),
            (-1, 1, in_side_behind),
            (1, 1, in_side_ahead),
            (2, 1, in_side_far),
        )
    )
    wide_out = in_order(
        (
            (0, 0, own_out),
            (0, 1, out_side),
            (-1, 0, out_behind),
            (1, 0, out_ahead),
            (2, 0, out_far),
            (-1, 1, out_side_behind),
            (1, 1, out_side_ahead),
            (2, 1, out_side_far),
        )
    )

    rows = rows.reshape(row_total, features + lanes)
    probs = rows[:, features:].astype(f32)
    lane = jnp.arange(lanes, dtype=jnp.int32)[None, :]
    weight = jnp.sum(
        jnp.where(lane == lax.axis_index("expert"), probs, 0.0), axis=1, keepdims=True
    )
    rows = rows[:, :features]
    preact = jnp.dot(rows, wide_in, preferred_element_type=f32)
    gate_value, up_value = preact[:, :hidden], preact[:, hidden:]
    gate_sigmoid = jax.nn.sigmoid(gate_value)
    silu_gate = gate_value * gate_sigmoid
    silu_slope = gate_sigmoid * (1.0 + gate_value * (1.0 - gate_sigmoid))
    activation = silu_gate * up_value
    scaled = after(
        (weight * activation).astype(bf16), out_side_far, out_side_behind, out_side_ahead
    )

    part_out = lax.dot_general(
        scaled, grads, (((0,), (0,)), ((), ())), preferred_element_type=f32
    ).astype(bf16)
    out_near = (
        along_z(chunk(part_out, 1, 1), 1),
        along_z(chunk(part_out, -1, 1), -1),
        along_z(chunk(part_out, 1, 0), 1),
        along_z(chunk(part_out, -1, 0), -1),
    )
    out_side_far = across_low(chunk(part_out, 2, 1))

    back_proj = lax.dot_general(
        grads, wide_out, (((1,), (1,)), ((), ())), preferred_element_type=f32
    )
    route_part = jnp.sum(activation * back_proj, axis=1).astype(bf16)
    act_grad = weight * back_proj
    pre_grad = jnp.concatenate(
        [act_grad * up_value * silu_slope, act_grad * silu_gate], axis=1
    ).astype(bf16)
    part_in = lax.dot_general(
        rows, pre_grad, (((0,), (0,)), ((), ())), preferred_element_type=f32
    ).astype(bf16)
    out_near, out_side_far, part_in, pre_grad = barrier(
        (out_near, out_side_far, part_in, pre_grad)
    )

    out_far = along_z(narrow(wide(chunk(part_out, 2, 0)) + wide(out_side_far)), 2)
    out_side = across_low(
        narrow(wide(chunk(part_out, 0, 1)) + wide(out_near[0]) + wide(out_near[1]))
    )
    side_halves = far_halves(part_in, 1)
    row_grad = lax.dot_general(
        pre_grad, wide_in, (((1,), (1,)), ((), ())), preferred_element_type=f32
    ).astype(bf16)
    sent_back = jnp.concatenate(
        [row_grad, jnp.broadcast_to(route_part[:, None], (row_total, lanes))], axis=1
    )
    back_rows = lax.all_to_all(
        sent_back.reshape(experts, slots, features + lanes),
        "expert",
        split_axis=0,
        concat_axis=0,
        tiled=True,
    )
    back_route = back_rows[:, :, features].astype(f32)
    out_far, out_side, side_halves, sent_back = barrier(
        (out_far, out_side, side_halves, sent_back)
    )
    grad_out = wide(chunk(part_out, 0, 0)) + wide(out_near[2]) + wide(out_near[3])
    grad_out = grad_out + wide(out_far) + wide(out_side)

    side_up, side_down = near_sums(part_in, 1, side_halves)
    side_near = along_z(side_up, 1), along_z(side_down, -1)
    own_halves = far_halves(part_in, 0)
    side_near, own_halves = barrier((side_near, own_halves))

    in_side = across_low(
        narrow(wide(chunk(part_in, 0, 1)) + wide(side_near[0]) + wide(side_near[1]))
    )
    own_up, own_down = near_sums(part_in, 0, own_halves)
    own_near = along_z(own_up, 1), along_z(own_down, -1)
    grad_in = wide(chunk(part_in, 0, 0)) + wide(own_near[0]) + wide(own_near[1]) + wide(in_side)

    input_grad = lax.dot_general(
        own_rows,
        back_rows[:, :, :features].reshape(row_total, features),
        (((0,), (0,)), ((), ())),
        preferred_element_type=f32,
    ).astype(bf16)
    by_token = jnp.sum(jnp.where(own_chosen, back_route[:, :, None], 0.0), axis=1)
    route_grad = jnp.sum(jnp.where(chose, by_token[None], 0.0), axis=1).T.astype(bf16)
    grad_in = after(grad_in, input_grad, route_grad)
    new_weights_out, new_first_out, new_second_out = adam_update(
        weights_out, first_out, second_out, grad_out[None]
    )
    new_weights_in, new_first_in, new_second_in = adam_update(
        weights_in, first_in, second_in, grad_in[None]
    )
    return (
        input_grad,
        route_grad,
        new_weights_in,
        new_weights_out,
        new_first_in,
        new_first_out,
        new_second_in,
        new_second_out,
    )


def solution(mesh):
    rows = P(("dp", "expert"), None)
    state = P("expert", "dp", None)
    return jax.shard_map(
        on_device,
        mesh=mesh,
        in_specs=(rows,) * 4 + (state,) * 6,
        out_specs=(rows,) * 2 + (state,) * 6,
        check_vma=False,
    )
```

```python
import jax
import jax.numpy as jnp
from jax import lax
from jax.experimental import pallas as pl
from jax.sharding import PartitionSpec as P

beta_one = 0.9
beta_two = 0.95
learn_rate = 0.00024
decay_rate = 0.1
adam_eps = 1e-08
adam_step = 100.0

ring = 4


def adam_update(weights, first, second, grad):
    first_new = beta_one * first + (1.0 - beta_one) * grad
    second_new = beta_two * second + (1.0 - beta_two) * grad * grad
    fix_one = 1.0 - beta_one**adam_step
    fix_two = 1.0 - beta_two**adam_step
    step_size = first_new / fix_one / (jnp.sqrt(second_new / fix_two) + adam_eps)
    return (weights - learn_rate * (step_size + decay_rate * weights), first_new, second_new)


def dp_at(index, dz, dy):
    return (index // 2 + dz) % ring * 2 + (index % 2 + dy) % 2


def dp_send(value, dz, dy):
    return lax.ppermute(value, "dp", [(i, dp_at(i, dz, dy)) for i in range(2 * ring)])


def ex_at(index, dy, dx, dc):
    return (index // 8 + dy) % 2 * 8 + (index // 2 + dx) % ring * 2 + (index + dc) % 2


def ex_send(value, dy, dx, dc):
    return lax.ppermute(value, "expert", [(i, ex_at(i, dy, dx, dc)) for i in range(4 * ring)])


def after(value, *others):
    return lax.optimization_barrier((value, *others))[0]


def along_z(value, step):
    return dp_send(value, step, 0)


def across_low(value):
    return dp_send(value, 0, 1)


def in_order(pieces):
    mine = lax.axis_index("dp")
    rows, columns = pieces[0][2].shape
    whole = pl.pallas_call(
        lambda out_ref: None,
        out_shape=jax.ShapeDtypeStruct((2 * ring * rows, columns), pieces[0][2].dtype),
        out_specs=pl.BlockSpec(memory_space=pl.ANY),
    )()
    for dz, dy, piece in pieces:
        whole = lax.dynamic_update_slice(whole, piece, (dp_at(mine, dz, dy) * rows, 0))
    return whole


def wide(value):
    return value.astype(jnp.float32)


def narrow(value):
    return value.astype(jnp.bfloat16)


def chunk(part, dz, dy, piece=None):
    rows = part.shape[0] // (2 * ring)
    place = dp_at(lax.axis_index("dp"), dz, dy) * rows
    if piece is not None:
        rows = rows // 2
        place = place + piece * rows
    return lax.dynamic_slice(part, (place, 0), (rows, part.shape[1]))


def far_halves(part, dy):
    return along_z(chunk(part, 2, dy, 0), 1), along_z(chunk(part, 2, dy, 1), -1)


def near_sums(part, dy, halves):
    up = jnp.concatenate(
        [narrow(wide(chunk(part, 1, dy, 0)) + wide(halves[0])), chunk(part, 1, dy, 1)], axis=0
    )
    down = jnp.concatenate(
        [chunk(part, -1, dy, 0), narrow(wide(chunk(part, -1, dy, 1)) + wide(halves[1]))], axis=0
    )
    return up, down


def on_device(
    tokens_in,
    out_grad,
    expert_ids,
    route_probs,
    weights_in,
    weights_out,
    first_in,
    first_out,
    second_in,
    second_out,
):
    experts = lax.axis_size("expert")
    token_count, top_count = expert_ids.shape
    features = tokens_in.shape[1]
    hidden = weights_out.shape[1] * lax.axis_size("dp")
    capacity = 9 * token_count * top_count // (8 * experts)
    slots = -(-capacity // 8) * 8
    f32, bf16 = jnp.float32, jnp.bfloat16

    chose = expert_ids.T[:, None, :] == jnp.arange(experts, dtype=jnp.int32)[None, :, None]
    sent_probs = jnp.sum(jnp.where(chose, route_probs.T[:, None, :].astype(f32), 0.0), axis=0)
    before = (
        jnp.arange(token_count)[:, None] < jnp.arange(token_count)[None, :]
    ).astype(bf16)

    def chosen_of(probs):
        chose_here = (probs > 0.0).astype(bf16)
        rank = lax.dot_general(
            chose_here, before, (((probs.ndim - 1,), (0,)), ((), ())), preferred_element_type=f32
        )
        slot = jnp.arange(slots, dtype=jnp.int32).astype(f32)[:, None]
        return (rank[..., None, :] == slot) & (probs[..., None, :] > 0.0)

    lanes = 128
    table = jnp.pad(sent_probs.astype(bf16).T, ((0, 0), (0, lanes - experts)))
    row_total = experts * slots
    own_chosen = chosen_of(sent_probs)
    own_rows = own_chosen.astype(bf16).reshape(row_total, token_count)

    half = experts // 2
    upper = lax.axis_index("expert") // half
    halves = [[low * half + i for i in range(half)] for low in range(2)]

    def picks_of(table_side):
        both = jnp.stack([sent_probs, table_side[:, :experts].astype(f32).T])
        both = lax.dynamic_slice(both, (0, upper * half, 0), (2, half, token_count))
        chosen = chosen_of(both).transpose(1, 0, 2, 3)
        place = jnp.arange(2, dtype=jnp.int32)
        source = (place[:, None] + upper) % 2 == jnp.arange(2, dtype=jnp.int32)[None, :]
        chosen = jnp.where(upper == 0, chosen, chosen[:, ::-1])
        chosen = chosen[:, :, :, None, :] & source[None, :, None, :, None]
        return chosen.astype(bf16).reshape(row_total, 2 * token_count)

    def pick(picks, values, values_side):
        picked = jnp.dot(
            picks, jnp.concatenate([values, values_side], axis=0), preferred_element_type=f32
        )
        return picked.astype(bf16).reshape(half, 2 * slots, values.shape[1])

    def exchange(picked):
        return lax.all_to_all(
            picked, "expert", split_axis=0, concat_axis=0, axis_index_groups=halves, tiled=True
        )

    barrier = lax.optimization_barrier
    own_in, own_out = weights_in[0].astype(bf16), weights_out[0].astype(bf16)
    token_side, table_side = ex_send(tokens_in, 1, 0, 0), ex_send(table, 1, 0, 0)
    in_behind, in_ahead = along_z(own_in, 1), along_z(own_in, -1)
    token_side, table_side, own_in, own_out, out_grad = barrier(
        (token_side, table_side, own_in, own_out, out_grad)
    )
    picks = picks_of(table_side)
    rows = exchange(
        pick(
            picks,
            jnp.concatenate([tokens_in, table], axis=1),
            jnp.concatenate([token_side, table_side], axis=1),
        )
    )
    in_far, in_side = along_z(own_in, 2), across_low(own_in)
    grad_side = ex_send(out_grad, 1, 0, 0)
    picked_grads = pick(picks, out_grad, grad_side)
    in_far, in_side, in_behind, in_ahead, picked_grads, rows, own_out = barrier(
        (in_far, in_side, in_behind, in_ahead, picked_grads, rows, own_out)
    )
    grads = exchange(picked_grads).reshape(row_total, features)
    in_side_behind, in_side_ahead = along_z(in_side, 1), along_z(in_side, -1)
    in_side_far = across_low(in_far)
    out_far, out_side = along_z(own_out, 2), across_low(own_out)
    in_side_behind, in_side_ahead, in_side_far, out_far, out_side, own_out = barrier(
        (in_side_behind, in_side_ahead, in_side_far, out_far, out_side, own_out)
    )
    out_behind, out_ahead = along_z(own_out, 1), along_z(own_out, -1)
    out_side_far = across_low(out_far)
    out_side_behind, out_side_ahead = along_z(out_side, 1), along_z(out_side, -1)
    wide_in = in_order(
        (
            (0, 0, own_in),
            (0, 1, in_side),
            (-1, 0, in_behind),
            (1, 0, in_ahead),
            (2, 0, in_far),
            (-1, 1, in_side_behind),
            (1, 1, in_side_ahead),
            (2, 1, in_side_far),
        )
    )
    wide_out = in_order(
        (
            (0, 0, own_out),
            (0, 1, out_side),
            (-1, 0, out_behind),
            (1, 0, out_ahead),
            (2, 0, out_far),
            (-1, 1, out_side_behind),
            (1, 1, out_side_ahead),
            (2, 1, out_side_far),
        )
    )

    rows = rows.reshape(row_total, features + lanes)
    probs = rows[:, features:].astype(f32)
    lane = jnp.arange(lanes, dtype=jnp.int32)[None, :]
    weight = jnp.sum(
        jnp.where(lane == lax.axis_index("expert"), probs, 0.0), axis=1, keepdims=True
    )
    rows = rows[:, :features]
    preact = jnp.dot(rows, wide_in, preferred_element_type=f32)
    gate_value, up_value = preact[:, :hidden], preact[:, hidden:]
    gate_sigmoid = jax.nn.sigmoid(gate_value)
    silu_gate = gate_value * gate_sigmoid
    silu_slope = gate_sigmoid * (1.0 + gate_value * (1.0 - gate_sigmoid))
    activation = silu_gate * up_value
    scaled = after(
        (weight * activation).astype(bf16),
        out_behind,
        out_ahead,
        out_side_far,
        out_side_behind,
        out_side_ahead,
    )

    part_out = lax.dot_general(
        scaled, grads, (((0,), (0,)), ((), ())), preferred_element_type=f32
    ).astype(bf16)
    out_near = (
        along_z(chunk(part_out, 1, 1), 1),
        along_z(chunk(part_out, -1, 1), -1),
        along_z(chunk(part_out, 1, 0), 1),
        along_z(chunk(part_out, -1, 0), -1),
    )
    out_side_far = across_low(chunk(part_out, 2, 1))

    back_proj = lax.dot_general(
        after(grads, part_out), wide_out, (((1,), (1,)), ((), ())), preferred_element_type=f32
    )
    route_part = jnp.sum(activation * back_proj, axis=1).astype(bf16)
    act_grad = weight * back_proj
    pre_grad = jnp.concatenate(
        [act_grad * up_value * silu_slope, act_grad * silu_gate], axis=1
    ).astype(bf16)
    row_grad = lax.dot_general(
        pre_grad, wide_in, (((1,), (1,)), ((), ())), preferred_element_type=f32
    ).astype(bf16)
    sent_back = jnp.concatenate(
        [row_grad, jnp.broadcast_to(route_part[:, None], (row_total, lanes))], axis=1
    )
    sent_back = sent_back.reshape(half, 2, slots, features + lanes).transpose(1, 0, 2, 3)
    sent_back = sent_back.reshape(experts, slots, features + lanes)
    back_rows = lax.all_to_all(sent_back, "expert", split_axis=0, concat_axis=0, tiled=True)
    out_near, out_side_far, sent_back, pre_grad = barrier(
        (out_near, out_side_far, sent_back, pre_grad)
    )

    out_far = along_z(narrow(wide(chunk(part_out, 2, 0)) + wide(out_side_far)), 2)
    out_side = across_low(
        narrow(wide(chunk(part_out, 0, 1)) + wide(out_near[0]) + wide(out_near[1]))
    )
    part_in = lax.dot_general(
        rows, pre_grad, (((0,), (0,)), ((), ())), preferred_element_type=f32
    ).astype(bf16)
    side_halves = far_halves(part_in, 1)
    out_far, side_halves = barrier((out_far, side_halves))
    side_up, side_down = near_sums(part_in, 1, side_halves)
    side_near = along_z(side_up, 1), along_z(side_down, -1)
    own_halves = far_halves(part_in, 0)
    side_near, own_halves, back_rows, out_side = barrier(
        (side_near, own_halves, back_rows, out_side)
    )
    grad_out = wide(chunk(part_out, 0, 0)) + wide(out_near[2]) + wide(out_near[3])
    grad_out = grad_out + wide(out_far) + wide(out_side)

    in_side = across_low(
        narrow(wide(chunk(part_in, 0, 1)) + wide(side_near[0]) + wide(side_near[1]))
    )
    own_up, own_down = near_sums(part_in, 0, own_halves)
    own_near = along_z(own_up, 1), along_z(own_down, -1)
    grad_in = wide(chunk(part_in, 0, 0)) + wide(own_near[0]) + wide(own_near[1]) + wide(in_side)

    back_route = back_rows[:, :, features].astype(f32)
    input_grad = lax.dot_general(
        own_rows,
        back_rows[:, :, :features].reshape(row_total, features),
        (((0,), (0,)), ((), ())),
        preferred_element_type=f32,
    ).astype(bf16)
    by_token = jnp.sum(jnp.where(own_chosen, back_route[:, :, None], 0.0), axis=1)
    route_grad = jnp.sum(jnp.where(chose, by_token[None], 0.0), axis=1).T.astype(bf16)
    new_weights_out, new_first_out, new_second_out = adam_update(
        weights_out, first_out, second_out, grad_out[None]
    )
    new_weights_in, new_first_in, new_second_in = adam_update(
        weights_in, first_in, second_in, grad_in[None]
    )
    return (
        input_grad,
        route_grad,
        new_weights_in,
        new_weights_out,
        new_first_in,
        new_first_out,
        new_second_in,
        new_second_out,
    )


def solution(mesh):
    rows = P(("dp", "expert"), None)
    state = P("expert", "dp", None)
    return jax.shard_map(
        on_device,
        mesh=mesh,
        in_specs=(rows,) * 4 + (state,) * 6,
        out_specs=(rows,) * 2 + (state,) * 6,
        check_vma=False,
    )
```

```python
import jax
import jax.numpy as jnp
from jax import lax
from jax.experimental import pallas as pl
from jax.sharding import PartitionSpec as P

beta_one = 0.9
beta_two = 0.95
learn_rate = 0.00024
decay_rate = 0.1
adam_eps = 1e-08
adam_step = 100.0

ring = 4


def adam_update(weights, first, second, grad):
    first_new = beta_one * first + (1.0 - beta_one) * grad
    second_new = beta_two * second + (1.0 - beta_two) * grad * grad
    fix_one = 1.0 - beta_one**adam_step
    fix_two = 1.0 - beta_two**adam_step
    step_size = first_new / fix_one / (jnp.sqrt(second_new / fix_two) + adam_eps)
    return (weights - learn_rate * (step_size + decay_rate * weights), first_new, second_new)


def dp_at(index, dz, dy):
    return (index // 2 + dz) % ring * 2 + (index % 2 + dy) % 2


def dp_send(value, dz, dy):
    return lax.ppermute(value, "dp", [(i, dp_at(i, dz, dy)) for i in range(2 * ring)])


def ex_at(index, dy, dx, dc):
    return (index // 8 + dy) % 2 * 8 + (index // 2 + dx) % ring * 2 + (index + dc) % 2


def ex_send(value, dy, dx, dc):
    return lax.ppermute(value, "expert", [(i, ex_at(i, dy, dx, dc)) for i in range(4 * ring)])


def after(value, *others):
    return lax.optimization_barrier((value, *others))[0]


def along_z(value, step):
    return dp_send(value, step, 0)


def across_low(value):
    return dp_send(value, 0, 1)


def blank(shape):
    return pl.pallas_call(
        lambda out_ref: None,
        out_shape=jax.ShapeDtypeStruct(shape, jnp.bfloat16),
        out_specs=pl.BlockSpec(memory_space=pl.ANY),
    )()


def in_order(pieces):
    mine = lax.axis_index("dp")
    rows, columns = pieces[0][2].shape
    whole = blank((2 * ring * rows, columns))
    for dz, dy, piece in pieces:
        whole = lax.dynamic_update_slice(whole, piece, (dp_at(mine, dz, dy) * rows, 0))
    return whole


def wide(value):
    return value.astype(jnp.float32)


def narrow(value):
    return value.astype(jnp.bfloat16)


def chunk(part, dz, dy, piece=None):
    rows = part.shape[0] // (2 * ring)
    place = dp_at(lax.axis_index("dp"), dz, dy) * rows
    if piece is not None:
        rows = rows // 2
        place = place + piece * rows
    return lax.dynamic_slice(part, (place, 0), (rows, part.shape[1]))


def far_halves(part, dy):
    return along_z(chunk(part, 2, dy, 0), 1), along_z(chunk(part, 2, dy, 1), -1)


def near_sums(part, dy, halves):
    up = jnp.concatenate(
        [narrow(wide(chunk(part, 1, dy, 0)) + wide(halves[0])), chunk(part, 1, dy, 1)], axis=0
    )
    down = jnp.concatenate(
        [chunk(part, -1, dy, 0), narrow(wide(chunk(part, -1, dy, 1)) + wide(halves[1]))], axis=0
    )
    return up, down


def on_device(
    tokens_in,
    out_grad,
    expert_ids,
    route_probs,
    weights_in,
    weights_out,
    first_in,
    first_out,
    second_in,
    second_out,
):
    experts = lax.axis_size("expert")
    token_count, top_count = expert_ids.shape
    features = tokens_in.shape[1]
    hidden = weights_out.shape[1] * lax.axis_size("dp")
    capacity = 9 * token_count * top_count // (8 * experts)
    slots = -(-capacity // 8) * 8
    f32, bf16 = jnp.float32, jnp.bfloat16

    chose = expert_ids.T[:, None, :] == jnp.arange(experts, dtype=jnp.int32)[None, :, None]
    sent_probs = jnp.sum(jnp.where(chose, route_probs.T[:, None, :].astype(f32), 0.0), axis=0)
    before = (
        jnp.arange(token_count)[:, None] < jnp.arange(token_count)[None, :]
    ).astype(bf16)

    def chosen_of(probs):
        chose_here = (probs > 0.0).astype(bf16)
        rank = lax.dot_general(
            chose_here, before, (((probs.ndim - 1,), (0,)), ((), ())), preferred_element_type=f32
        )
        slot = jnp.arange(slots, dtype=jnp.int32).astype(f32)[:, None]
        return (rank[..., None, :] == slot) & (probs[..., None, :] > 0.0)

    lanes = 128
    table = jnp.pad(sent_probs.astype(bf16).T, ((0, 0), (0, lanes - experts)))
    row_total = experts * slots
    half = experts // 2
    upper = lax.axis_index("expert") // half
    halves = [[low * half + i for i in range(half)] for low in range(2)]

    def half_chosen(probs):
        return chosen_of(lax.dynamic_slice(probs, (upper * half, 0), (half, token_count)))

    def pick(chosen, values):
        chosen = chosen.reshape(-1, chosen.shape[-1])
        picked = jnp.dot(chosen, values, preferred_element_type=f32)
        return picked.astype(bf16).reshape(half, -1, values.shape[1])

    def exchange(picked):
        return lax.all_to_all(
            picked, "expert", split_axis=0, concat_axis=0, axis_index_groups=halves, tiled=True
        )

    barrier = lax.optimization_barrier
    own_in, own_out = weights_in[0].astype(bf16), weights_out[0].astype(bf16)
    token_side, table_side = ex_send(tokens_in, 1, 0, 0), ex_send(table, 1, 0, 0)
    in_behind, in_ahead, in_side = along_z(own_in, 1), along_z(own_in, -1), across_low(own_in)
    chosen_own = half_chosen(sent_probs)
    rows_own = exchange(pick(chosen_own.astype(bf16), jnp.concatenate([tokens_in, table], axis=1)))
    chosen_side = half_chosen(table_side[:, :experts].astype(f32).T)
    picked_side = pick(
        chosen_side.astype(bf16), jnp.concatenate([token_side, table_side], axis=1)
    )
    picked_side, rows_own, own_in, own_out, out_grad = barrier(
        (picked_side, rows_own, own_in, own_out, out_grad)
    )
    rows_side = exchange(picked_side)
    in_far, out_side, grad_side = along_z(own_in, 2), across_low(own_out), ex_send(out_grad, 1, 0, 0)
    source = (jnp.arange(2)[:, None] + upper) % 2 == jnp.arange(2)[None, :]
    first = jnp.where(upper == 0, chosen_own, chosen_side)
    second = jnp.where(upper == 0, chosen_side, chosen_own)
    chosen_both = jnp.stack([first, second], axis=1)[:, :, :, None, :]
    chosen_both = (chosen_both & source[None, :, None, :, None]).astype(bf16)
    picks = chosen_both.reshape(row_total, 2 * token_count)
    picked_grads = pick(picks, jnp.concatenate([out_grad, grad_side], axis=0))
    in_behind, in_ahead, in_far, out_side, picked_grads, rows_side, in_side, own_out = barrier(
        (in_behind, in_ahead, in_far, out_side, picked_grads, rows_side, in_side, own_out)
    )
    rows = blank((half, 2, slots, features + lanes))
    rows = lax.dynamic_update_slice(rows, rows_own[:, None], (0, upper, 0, 0))
    rows = lax.dynamic_update_slice(rows, rows_side[:, None], (0, 1 - upper, 0, 0))
    grads = exchange(picked_grads).reshape(row_total, features)
    in_side_behind, in_side_ahead = along_z(in_side, 1), along_z(in_side, -1)
    in_side_far = across_low(in_far)
    out_far = along_z(own_out, 2)
    in_side_behind, in_side_ahead, in_side_far, out_far, own_out, out_side = barrier(
        (in_side_behind, in_side_ahead, in_side_far, out_far, own_out, out_side)
    )
    out_behind, out_ahead = along_z(own_out, 1), along_z(own_out, -1)
    out_side_far = across_low(out_far)
    out_side_behind, out_side_ahead = along_z(out_side, 1), along_z(out_side, -1)
    wide_in = in_order(
        (
            (0, 0, own_in),
            (0, 1, in_side),
            (-1, 0, in_behind),
            (1, 0, in_ahead),
            (2, 0, in_far),
            (-1, 1, in_side_behind),
            (1, 1, in_side_ahead),
            (2, 1, in_side_far),
        )
    )
    wide_out = in_order(
        (
            (0, 0, own_out),
            (0, 1, out_side),
            (-1, 0, out_behind),
            (1, 0, out_ahead),
            (2, 0, out_far),
            (-1, 1, out_side_behind),
            (1, 1, out_side_ahead),
            (2, 1, out_side_far),
        )
    )

    rows = rows.reshape(row_total, features + lanes)
    probs = rows[:, features:].astype(f32)
    lane = jnp.arange(lanes, dtype=jnp.int32)[None, :]
    weight = jnp.sum(
        jnp.where(lane == lax.axis_index("expert"), probs, 0.0), axis=1, keepdims=True
    )
    rows = rows[:, :features]
    preact = jnp.dot(rows, wide_in, preferred_element_type=f32)
    gate_value, up_value = preact[:, :hidden], preact[:, hidden:]
    gate_sigmoid = jax.nn.sigmoid(gate_value)
    silu_gate = gate_value * gate_sigmoid
    silu_slope = gate_sigmoid * (1.0 + gate_value * (1.0 - gate_sigmoid))
    activation = silu_gate * up_value
    scaled = after(
        (weight * activation).astype(bf16),
        out_behind,
        out_ahead,
        out_side_far,
        out_side_behind,
        out_side_ahead,
    )

    part_out = lax.dot_general(
        scaled, grads, (((0,), (0,)), ((), ())), preferred_element_type=f32
    ).astype(bf16)
    out_near = (
        along_z(chunk(part_out, 1, 1), 1),
        along_z(chunk(part_out, -1, 1), -1),
        along_z(chunk(part_out, 1, 0), 1),
        along_z(chunk(part_out, -1, 0), -1),
    )
    out_side_far = across_low(chunk(part_out, 2, 1))

    back_proj = lax.dot_general(
        after(grads, part_out), wide_out, (((1,), (1,)), ((), ())), preferred_element_type=f32
    )
    route_part = jnp.sum(activation * back_proj, axis=1).astype(bf16)
    act_grad = weight * back_proj
    pre_grad = jnp.concatenate(
        [act_grad * up_value * silu_slope, act_grad * silu_gate], axis=1
    ).astype(bf16)
    part_in = lax.dot_general(
        rows, pre_grad, (((0,), (0,)), ((), ())), preferred_element_type=f32
    ).astype(bf16)
    out_near, out_side_far, part_in, pre_grad = barrier(
        (out_near, out_side_far, part_in, pre_grad)
    )

    out_far = along_z(narrow(wide(chunk(part_out, 2, 0)) + wide(out_side_far)), 2)
    out_side = across_low(
        narrow(wide(chunk(part_out, 0, 1)) + wide(out_near[0]) + wide(out_near[1]))
    )
    side_halves = far_halves(part_in, 1)
    row_grad = lax.dot_general(
        pre_grad, wide_in, (((1,), (1,)), ((), ())), preferred_element_type=f32
    ).astype(bf16)
    route_lanes = jnp.where(lane == lax.axis_index("expert"), route_part[:, None], 0)
    sent_back = jnp.concatenate([row_grad, route_lanes.astype(bf16)], axis=1)
    back_rows = exchange(sent_back.reshape(half, 2 * slots, features + lanes))
    out_far, out_side, side_halves, _ = barrier((out_far, out_side, side_halves, sent_back))
    side_up, side_down = near_sums(part_in, 1, side_halves)
    side_near = along_z(side_up, 1), along_z(side_down, -1)
    own_halves = far_halves(part_in, 0)
    side_near, own_halves = barrier((side_near, own_halves))
    grad_out = wide(chunk(part_out, 0, 0)) + wide(out_near[2]) + wide(out_near[3])
    grad_out = grad_out + wide(out_far) + wide(out_side)

    in_side = across_low(
        narrow(wide(chunk(part_in, 0, 1)) + wide(side_near[0]) + wide(side_near[1]))
    )
    own_up, own_down = near_sums(part_in, 0, own_halves)
    own_near = along_z(own_up, 1), along_z(own_down, -1)
    grad_in = wide(chunk(part_in, 0, 0)) + wide(own_near[0]) + wide(own_near[1]) + wide(in_side)

    sums = lax.dot_general(
        picks,
        back_rows.reshape(row_total, features + lanes),
        (((0,), (0,)), ((), ())),
        preferred_element_type=f32,
    )
    sums = sums[:token_count] + wide(ex_send(narrow(sums[token_count:]), 1, 0, 0))
    input_grad = narrow(sums[:, :features])
    by_token = sums[:, features : features + experts].T
    route_grad = jnp.sum(jnp.where(chose, by_token[None], 0.0), axis=1).T.astype(bf16)
    new_weights_out, new_first_out, new_second_out = adam_update(
        weights_out, first_out, second_out, grad_out[None]
    )
    new_weights_in, new_first_in, new_second_in = adam_update(
        weights_in, first_in, second_in, grad_in[None]
    )
    return (
        input_grad,
        route_grad,
        new_weights_in,
        new_weights_out,
        new_first_in,
        new_first_out,
        new_second_in,
        new_second_out,
    )


def solution(mesh):
    rows = P(("dp", "expert"), None)
    state = P("expert", "dp", None)
    return jax.shard_map(
        on_device,
        mesh=mesh,
        in_specs=(rows,) * 4 + (state,) * 6,
        out_specs=(rows,) * 2 + (state,) * 6,
        check_vma=False,
    )
```

```python
import jax
import jax.numpy as jnp
from jax import lax
from jax.experimental import pallas as pl
from jax.sharding import PartitionSpec as P

beta_one = 0.9
beta_two = 0.95
learn_rate = 0.00024
decay_rate = 0.1
adam_eps = 1e-08
adam_step = 100.0

ring = 4


def adam_update(weights, first, second, grad):
    first_new = beta_one * first + (1.0 - beta_one) * grad
    second_new = beta_two * second + (1.0 - beta_two) * grad * grad
    fix_one = 1.0 - beta_one**adam_step
    fix_two = 1.0 - beta_two**adam_step
    step_size = first_new / fix_one / (jnp.sqrt(second_new / fix_two) + adam_eps)
    return (weights - learn_rate * (step_size + decay_rate * weights), first_new, second_new)


def dp_at(index, dz, dy):
    return (index // 2 + dz) % ring * 2 + (index % 2 + dy) % 2


def dp_send(value, dz, dy):
    return lax.ppermute(value, "dp", [(i, dp_at(i, dz, dy)) for i in range(2 * ring)])


def ex_at(index, dy, dx, dc):
    return (index // 8 + dy) % 2 * 8 + (index // 2 + dx) % ring * 2 + (index + dc) % 2


def ex_send(value, dy, dx, dc):
    return lax.ppermute(value, "expert", [(i, ex_at(i, dy, dx, dc)) for i in range(4 * ring)])


def after(value, *others):
    return lax.optimization_barrier((value, *others))[0]


def along_z(value, step):
    return dp_send(value, step, 0)


def across_low(value):
    return dp_send(value, 0, 1)


def blank(shape):
    return pl.pallas_call(
        lambda out_ref: None,
        out_shape=jax.ShapeDtypeStruct(shape, jnp.bfloat16),
        out_specs=pl.BlockSpec(memory_space=pl.ANY),
    )()


def in_order(pieces):
    mine = lax.axis_index("dp")
    rows, columns = pieces[0][2].shape
    whole = blank((2 * ring * rows, columns))
    for dz, dy, piece in pieces:
        whole = lax.dynamic_update_slice(whole, piece, (dp_at(mine, dz, dy) * rows, 0))
    return whole


def wide(value):
    return value.astype(jnp.float32)


def narrow(value):
    return value.astype(jnp.bfloat16)


def chunk(part, dz, dy, piece=None):
    rows = part.shape[0] // (2 * ring)
    place = dp_at(lax.axis_index("dp"), dz, dy) * rows
    if piece is not None:
        rows = rows // 2
        place = place + piece * rows
    return lax.dynamic_slice(part, (place, 0), (rows, part.shape[1]))


def far_halves(part, dy):
    return along_z(chunk(part, 2, dy, 0), 1), along_z(chunk(part, 2, dy, 1), -1)


def near_sums(part, dy, halves):
    up = jnp.concatenate(
        [narrow(wide(chunk(part, 1, dy, 0)) + wide(halves[0])), chunk(part, 1, dy, 1)], axis=0
    )
    down = jnp.concatenate(
        [chunk(part, -1, dy, 0), narrow(wide(chunk(part, -1, dy, 1)) + wide(halves[1]))], axis=0
    )
    return up, down


def on_device(
    tokens_in,
    out_grad,
    expert_ids,
    route_probs,
    weights_in,
    weights_out,
    first_in,
    first_out,
    second_in,
    second_out,
):
    experts = lax.axis_size("expert")
    token_count, top_count = expert_ids.shape
    features = tokens_in.shape[1]
    hidden = weights_out.shape[1] * lax.axis_size("dp")
    capacity = 9 * token_count * top_count // (8 * experts)
    slots = -(-capacity // 8) * 8
    f32, bf16 = jnp.float32, jnp.bfloat16

    chose = expert_ids.T[:, None, :] == jnp.arange(experts, dtype=jnp.int32)[None, :, None]
    sent_probs = jnp.sum(jnp.where(chose, route_probs.T[:, None, :].astype(f32), 0.0), axis=0)
    before = (
        jnp.arange(token_count)[:, None] < jnp.arange(token_count)[None, :]
    ).astype(bf16)

    def chosen_of(probs):
        chose_here = (probs > 0.0).astype(bf16)
        rank = lax.dot_general(
            chose_here, before, (((probs.ndim - 1,), (0,)), ((), ())), preferred_element_type=f32
        )
        slot = jnp.arange(slots, dtype=jnp.int32).astype(f32)[:, None]
        return (rank[..., None, :] == slot) & (probs[..., None, :] > 0.0)

    lanes = 128
    table = jnp.pad(sent_probs.astype(bf16).T, ((0, 0), (0, lanes - experts)))
    row_total = experts * slots
    half = experts // 2
    upper = lax.axis_index("expert") // half
    halves = [[low * half + i for i in range(half)] for low in range(2)]

    def half_chosen(probs):
        return chosen_of(lax.dynamic_slice(probs, (upper * half, 0), (half, token_count)))

    def pick(chosen, values):
        chosen = chosen.reshape(-1, chosen.shape[-1])
        picked = jnp.dot(chosen, values, preferred_element_type=f32)
        return picked.astype(bf16).reshape(half, -1, values.shape[1])

    def exchange(picked):
        return lax.all_to_all(
            picked, "expert", split_axis=0, concat_axis=0, axis_index_groups=halves, tiled=True
        )

    barrier = lax.optimization_barrier
    own_in, own_out = weights_in[0].astype(bf16), weights_out[0].astype(bf16)
    token_side, table_side = ex_send(tokens_in, 1, 0, 0), ex_send(table, 1, 0, 0)
    in_behind, in_ahead, in_side = along_z(own_in, 1), along_z(own_in, -1), across_low(own_in)
    chosen_own = half_chosen(sent_probs)
    rows_own = exchange(pick(chosen_own.astype(bf16), jnp.concatenate([tokens_in, table], axis=1)))
    chosen_side = half_chosen(table_side[:, :experts].astype(f32).T)
    picked_side = pick(
        chosen_side.astype(bf16), jnp.concatenate([token_side, table_side], axis=1)
    )
    picked_side, rows_own, own_in, own_out, out_grad = barrier(
        (picked_side, rows_own, own_in, own_out, out_grad)
    )
    rows_side = exchange(picked_side)
    in_far, out_side, grad_side = along_z(own_in, 2), across_low(own_out), ex_send(out_grad, 1, 0, 0)
    source = (jnp.arange(2)[:, None] + upper) % 2 == jnp.arange(2)[None, :]
    first = jnp.where(upper == 0, chosen_own, chosen_side)
    second = jnp.where(upper == 0, chosen_side, chosen_own)
    chosen_both = jnp.stack([first, second], axis=1)[:, :, :, None, :]
    chosen_both = (chosen_both & source[None, :, None, :, None]).astype(bf16)
    picks = chosen_both.reshape(row_total, 2 * token_count)
    picked_grads = pick(picks, jnp.concatenate([out_grad, grad_side], axis=0))
    in_behind, in_ahead, in_far, out_side, picked_grads, rows_side, in_side, own_out = barrier(
        (in_behind, in_ahead, in_far, out_side, picked_grads, rows_side, in_side, own_out)
    )
    rows = blank((half, 2, slots, features + lanes))
    rows = lax.dynamic_update_slice(rows, rows_own[:, None], (0, upper, 0, 0))
    rows = lax.dynamic_update_slice(rows, rows_side[:, None], (0, 1 - upper, 0, 0))
    grads = exchange(picked_grads).reshape(row_total, features)
    in_side_behind, in_side_ahead = along_z(in_side, 1), along_z(in_side, -1)
    in_side_far = across_low(in_far)
    out_far = along_z(own_out, 2)
    in_side_behind, in_side_ahead, in_side_far, out_far, own_out, out_side = barrier(
        (in_side_behind, in_side_ahead, in_side_far, out_far, own_out, out_side)
    )
    out_behind, out_ahead = along_z(own_out, 1), along_z(own_out, -1)
    out_side_far = across_low(out_far)
    out_side_behind, out_side_ahead = along_z(out_side, 1), along_z(out_side, -1)
    wide_in = in_order(
        (
            (0, 0, own_in),
            (0, 1, in_side),
            (-1, 0, in_behind),
            (1, 0, in_ahead),
            (2, 0, in_far),
            (-1, 1, in_side_behind),
            (1, 1, in_side_ahead),
            (2, 1, in_side_far),
        )
    )
    wide_out = in_order(
        (
            (0, 0, own_out),
            (0, 1, out_side),
            (-1, 0, out_behind),
            (1, 0, out_ahead),
            (2, 0, out_far),
            (-1, 1, out_side_behind),
            (1, 1, out_side_ahead),
            (2, 1, out_side_far),
        )
    )

    rows = rows.reshape(row_total, features + lanes)
    probs = rows[:, features:].astype(f32)
    lane = jnp.arange(lanes, dtype=jnp.int32)[None, :]
    weight = jnp.sum(
        jnp.where(lane == lax.axis_index("expert"), probs, 0.0), axis=1, keepdims=True
    )
    rows = rows[:, :features]
    preact = jnp.dot(rows, wide_in, preferred_element_type=f32)
    gate_value, up_value = preact[:, :hidden], preact[:, hidden:]
    gate_sigmoid = jax.nn.sigmoid(gate_value)
    silu_gate = gate_value * gate_sigmoid
    silu_slope = gate_sigmoid * (1.0 + gate_value * (1.0 - gate_sigmoid))
    activation = silu_gate * up_value
    scaled = after(
        (weight * activation).astype(bf16),
        out_behind,
        out_ahead,
        out_side_behind,
        out_side_ahead,
    )

    part_out = lax.dot_general(
        scaled, grads, (((0,), (0,)), ((), ())), preferred_element_type=f32
    ).astype(bf16)
    out_near = (
        along_z(chunk(part_out, 1, 1), 1),
        along_z(chunk(part_out, -1, 1), -1),
        along_z(chunk(part_out, 1, 0), 1),
        along_z(chunk(part_out, -1, 0), -1),
    )
    out_side_far = across_low(chunk(part_out, 2, 1))

    back_proj = lax.dot_general(
        after(grads, part_out), wide_out, (((1,), (1,)), ((), ())), preferred_element_type=f32
    )
    route_part = jnp.sum(activation * back_proj, axis=1).astype(bf16)
    act_grad = weight * back_proj
    pre_grad = jnp.concatenate(
        [act_grad * up_value * silu_slope, act_grad * silu_gate], axis=1
    ).astype(bf16)
    part_in = lax.dot_general(
        rows, pre_grad, (((0,), (0,)), ((), ())), preferred_element_type=f32
    ).astype(bf16)
    out_near, out_side_far, part_in, pre_grad = barrier(
        (out_near, out_side_far, part_in, pre_grad)
    )

    out_far = along_z(narrow(wide(chunk(part_out, 2, 0)) + wide(out_side_far)), 2)
    out_side = across_low(
        narrow(wide(chunk(part_out, 0, 1)) + wide(out_near[0]) + wide(out_near[1]))
    )
    side_halves = far_halves(part_in, 1)
    row_grad = lax.dot_general(
        pre_grad, wide_in, (((1,), (1,)), ((), ())), preferred_element_type=f32
    ).astype(bf16)
    route_lanes = jnp.where(lane == lax.axis_index("expert"), route_part[:, None], 0)
    sent_back = jnp.concatenate([row_grad, route_lanes.astype(bf16)], axis=1)
    back_rows = exchange(sent_back.reshape(half, 2 * slots, features + lanes))
    out_far, out_side, side_halves, _ = barrier((out_far, out_side, side_halves, sent_back))
    side_up, side_down = near_sums(part_in, 1, side_halves)
    side_near = along_z(side_up, 1), along_z(side_down, -1)
    own_halves = far_halves(part_in, 0)
    side_near, own_halves = barrier((side_near, own_halves))
    grad_out = wide(chunk(part_out, 0, 0)) + wide(out_near[2]) + wide(out_near[3])
    grad_out = grad_out + wide(out_far) + wide(out_side)

    in_side = across_low(
        narrow(wide(chunk(part_in, 0, 1)) + wide(side_near[0]) + wide(side_near[1]))
    )
    own_up, own_down = near_sums(part_in, 0, own_halves)
    own_near = along_z(own_up, 1), along_z(own_down, -1)
    grad_in = wide(chunk(part_in, 0, 0)) + wide(own_near[0]) + wide(own_near[1]) + wide(in_side)

    sums = lax.dot_general(
        picks,
        back_rows.reshape(row_total, features + lanes),
        (((0,), (0,)), ((), ())),
        preferred_element_type=f32,
    )
    sums = sums[:token_count] + wide(ex_send(narrow(sums[token_count:]), 1, 0, 0))
    input_grad = narrow(sums[:, :features])
    by_token = sums[:, features : features + experts].T
    route_grad = jnp.sum(jnp.where(chose, by_token[None], 0.0), axis=1).T.astype(bf16)
    new_weights_out, new_first_out, new_second_out = adam_update(
        weights_out, first_out, second_out, grad_out[None]
    )
    new_weights_in, new_first_in, new_second_in = adam_update(
        weights_in, first_in, second_in, grad_in[None]
    )
    return (
        input_grad,
        route_grad,
        new_weights_in,
        new_weights_out,
        new_first_in,
        new_first_out,
        new_second_in,
        new_second_out,
    )


def solution(mesh):
    rows = P(("dp", "expert"), None)
    state = P("expert", "dp", None)
    return jax.shard_map(
        on_device,
        mesh=mesh,
        in_specs=(rows,) * 4 + (state,) * 6,
        out_specs=(rows,) * 2 + (state,) * 6,
        check_vma=False,
    )
```
